32 devices in a mesh: groups: 2 (over x), blk: 4 (over y, core), ref: 4 (over z).
Axes of the slice: x: 2, y: 2, z: 4, core: 2. Of those that a mesh axis runs over, the one named last changes fastest.
Arguments:
- queries: bfloat16 [4096, 1024], P(('groups', 'blk')), parts along dimension 0, may hold values from -4 to 4
- references: bfloat16 [8192, 1024], P(('groups', 'blk', 'ref')), parts along dimension 0, may hold values from -4 to 4
- labels: bfloat16 [8192, 512], P(('groups', 'blk', 'ref')), parts along dimension 0, may hold values from 0.0009994507 to 1
Outputs:
- log_scores: float32 [4096, 512], P(('groups', 'blk', 'ref')), parts along dimension 0
The draws below stay inside these ranges and needn't reach their ends.
There are 2 independent parts, one for each index of `groups`. The reference program is written for one: setup_inputs(seed, part) draws one part's arguments, and reference() takes and returns one part's arrays. A program takes and returns all parts, laid end to end along the dimension named above; each array names one. Nothing has to cross between parts.
All inputs are finite; a program needn't handle non-finite values.
Results may differ from the reference program's by a relative error of at most 0.007.
Values may be sent and summed in bfloat16 or wider, within the bound.
A program may use at most 128 MiB of HBM per device.

```python
import math
import jax
import jax.numpy as jnp
from jax import lax

E = 1024
C = 512
Q_DEV = 512
NQ = 2048
NR = 4096


def draw_pair(key):
    base_key = jax.random.fold_in(key, 7)
    subkeys = jax.random.split(base_key, 2)
    queries = jnp.clip(jax.random.normal(subkeys[0], (NQ, E), jnp.float32), -4.0, 4.0)
    references = jnp.clip(jax.random.normal(subkeys[1], (NR, E), jnp.float32), -4.0, 4.0)
    return (queries.astype(jnp.bfloat16), references.astype(jnp.bfloat16))


def draw_queries(key, part):
    return draw_pair(key)[0]


def draw_references(key, part):
    return draw_pair(key)[1]


def level_of(stream_key, extent, cuts, least, top_value):
    loudness = 1.0
    for position, parts in cuts:
        steps = jax.random.uniform(jax.random.fold_in(jax.random.fold_in(stream_key, 6), position), (parts,), jnp.float32, least / len(cuts), top_value / len(cuts))
        loudness = loudness * jnp.repeat(jnp.exp(steps), extent[position] // parts).reshape((-1,) + (1,) * (len(extent) - 1 - position))
    return loudness


def setup_inputs(seed: int = 0, part: int = 0) -> dict:
    keys = jax.random.split(jax.random.key(seed), 4)
    own_keys = jax.random.split(jax.random.fold_in(keys[3], part), 4)
    return {
        "queries": draw_queries(jax.random.fold_in(jax.random.fold_in(keys[3], part), 71), part),
        "references": draw_references(jax.random.fold_in(jax.random.fold_in(keys[3], part), 71), part),
        "labels": jnp.clip(jnp.exp(math.log(1.0) - 6.9083047 * jax.random.uniform(own_keys[2], (NR, C), jnp.float32) ** level_of(own_keys[2], (NR, C), ((0, 16),), -0.2, 0.2)), 0.0009994507, 1.0).astype(jnp.bfloat16),
    }


def reference(queries, references, labels):
    width = queries.shape[1]
    classes = labels.shape[1]
    score_scale = 2.0 / math.sqrt(width)
    blocked = queries.reshape(NQ // Q_DEV, Q_DEV, width)

    def one_block(members):
        scores = jnp.dot(members, references.T, preferred_element_type=jnp.float32) * score_scale
        row_top = lax.optimization_barrier(jnp.max(scores, axis=1))
        weights = jnp.exp(scores - row_top[:, None]).astype(jnp.bfloat16)
        row_total = lax.optimization_barrier(jnp.sum(weights.astype(jnp.float32), axis=1))
        row_mass = jnp.dot(weights, labels, preferred_element_type=jnp.float32)
        return jnp.log(row_mass) - jnp.log(row_total)[:, None]
    return lax.map(one_block, blocked).reshape(NQ, classes)
```

```python
import functools
import math

import jax
import jax.numpy as jnp
from jax import lax
from jax.experimental import pallas as pl
from jax.experimental.pallas import tpu as pltpu
from jax.sharding import PartitionSpec as P

MESH = pl.DeviceIdType.MESH
LANES = 128
VMEM_LIMIT = 52 * 1024 * 1024


def kernel(
    ny, cores, nz, score_scale,
    q_hbm, r_hbm, l_hbm, out_ref,
    q, refs, labs, scores, peak, wts, mass, stage, landed, stat_out, stat_in, wide,
    q_sem, own_sem, send_sem, recv_sem, zsend_sem, zrecv_sem, tsend_sem, trecv_sem,
):
    blk = lax.axis_index("blk")
    zi = lax.axis_index("ref")
    nb = ny * cores
    rows, width = r_hbm.shape
    classes = l_hbm.shape[1]
    nq = q_hbm.shape[0]
    share = nq // nz
    nr = rows // LANES
    nc = classes // LANES
    items = nr + nc
    yi, core = blk // cores, blk % cores
    sibling = yi * cores + (1 - core)

    def peer(d):
        return ((yi + d) % ny) * cores + core

    def zpeer(d):
        return (zi + d) % nz

    def ref_piece(slot, j):
        return refs.at[slot, pl.ds(pl.multiple_of(j * LANES, LANES), LANES)]

    def lab_piece(slot, c):
        return labs.at[c, pl.ds(pl.multiple_of(slot * rows, rows), rows)]

    def own_ref(j):
        return r_hbm.at[pl.ds(j * LANES, LANES)]

    def own_lab(c):
        return l_hbm.at[:, pl.ds(c * LANES, LANES)]

    def remote(src, dst, sent, slot, item, dev):
        return pltpu.make_async_remote_copy(
            src_ref=src, dst_ref=dst, send_sem=send_sem.at[sent, item], recv_sem=recv_sem.at[slot, item],
            device_id={"blk": dev}, device_id_type=MESH,
        )

    def to_peer_ref(d, j):
        slot = cores * (ny - d)
        return remote(own_ref(j), ref_piece(slot, j), cores * d, slot, j, peer(d))

    def to_peer_lab(d, c):
        slot = cores * (ny - d)
        return remote(own_lab(c), lab_piece(slot, c), cores * d, slot, nr + c, peer(d))

    def to_sib_ref(j):
        return remote(own_ref(j), ref_piece(1, j), 1, 1, j, sibling)

    def to_sib_lab(c):
        return remote(own_lab(c), lab_piece(1, c), 1, 1, nr + c, sibling)

    def pass_ref(d, j):
        return remote(ref_piece(cores * d, j), ref_piece(cores * d + 1, j), cores * d + 1, cores * d + 1, j, sibling)

    def pass_lab(d, c):
        return remote(lab_piece(cores * d, c), lab_piece(cores * d + 1, c), cores * d + 1, cores * d + 1, nr + c, sibling)

    def arrived_ref(slot, j):
        remote(ref_piece(slot, j), ref_piece(slot, j), slot, slot, j, sibling).wait_recv()

    def arrived_lab(slot, c):
        remote(lab_piece(slot, c), lab_piece(slot, c), slot, slot, nr + c, sibling).wait_recv()

    q_copy = pltpu.make_async_copy(q_hbm, q, q_sem)
    q_copy.start()
    own_copies = [pltpu.make_async_copy(own_ref(j), ref_piece(0, j), own_sem.at[j]) for j in range(nr)]
    own_copies += [pltpu.make_async_copy(own_lab(c), lab_piece(0, c), own_sem.at[nr + c]) for c in range(nc)]
    for copy in own_copies:
        copy.start()

    barrier = pltpu.get_barrier_semaphore()
    if cores == 2:
        pl.semaphore_signal(barrier, inc=1, device_id={"blk": sibling}, device_id_type=MESH)
    for d in range(1, ny):
        pl.semaphore_signal(barrier, inc=1, device_id={"blk": peer(d)}, device_id_type=MESH)
    for d in range(1, nz):
        pl.semaphore_signal(barrier, inc=1, device_id={"ref": zpeer(d)}, device_id_type=MESH)
    pl.semaphore_wait(barrier, cores - 1 + ny - 1 + nz - 1)

    for j in range(nr):
        for d in range(1, ny):
            to_peer_ref(d, j).start()
    if cores == 2:
        for j in range(nr):
            to_sib_ref(j).start()
    for c in range(nc):
        for d in range(1, ny):
            to_peer_lab(d, c).start()
    if cores == 2:
        for c in range(nc):
            to_sib_lab(c).start()

    peak[...] = jnp.full(peak.shape, -jnp.inf, jnp.float32)

    def score(slot, j):
        part = lax.dot_general(
            q[...], ref_piece(slot, j)[...], (((1,), (1,)), ((), ())), preferred_element_type=jnp.float32
        ) * score_scale
        scores[slot * nr + j] = part
        peak[...] = jnp.maximum(peak[...], part)

    q_copy.wait()
    for j in range(nr):
        own_copies[j].wait()

    def own_step(j, carry):
        score(0, j)
        return carry

    lax.fori_loop(0, nr, own_step, 0)

    if cores == 2:

        def sib_step(j, carry):
            arrived_ref(1, j)
            score(1, j)
            return carry

        lax.fori_loop(0, nr, sib_step, 0)

    def far_step(i, carry):
        d, j = 1 + i // nr, i % nr
        arrived_ref(cores * d, j)
        if cores == 2:
            pass_ref(d, j).start()
        score(cores * d, j)
        if cores == 2:
            arrived_ref(cores * d + 1, j)
            score(cores * d + 1, j)
        return carry

    lax.fori_loop(0, (ny - 1) * nr, far_step, 0)

    lane = lax.broadcasted_iota(jnp.int32, (LANES, LANES), 1)

    def weigh(t, carry):
        r = pl.ds(pl.multiple_of(t * LANES, LANES), LANES)
        top = jnp.broadcast_to(jnp.max(peak[r, :], axis=1, keepdims=True), (LANES, LANES))

        def one(i, total):
            w = jnp.exp(scores[i, r, :] - top).astype(jnp.bfloat16)
            wts[r, pl.ds(pl.multiple_of(i * LANES, LANES), LANES)] = w
            return total + w.astype(jnp.float32)

        total = lax.fori_loop(0, nb * nr, one, jnp.zeros((LANES, LANES), jnp.float32), unroll=nb * nr <= 8)
        total = jnp.broadcast_to(jnp.sum(total, axis=1, keepdims=True), (LANES, LANES))
        stat_out[:, r] = jnp.where(lane < 4, top, total).T[0:8]
        return carry

    lax.fori_loop(0, nq // LANES, weigh, 0)

    narrow = share % LANES == 0

    def stat_copy(d):
        to = zpeer(d)
        src = stat_out.at[:, pl.ds(pl.multiple_of(to * share, LANES), share)] if narrow else stat_out
        return pltpu.make_async_remote_copy(
            src_ref=src, dst_ref=stat_in.at[nz - d], send_sem=tsend_sem.at[d], recv_sem=trecv_sem.at[nz - d],
            device_id={"ref": to}, device_id_type=MESH,
        )

    def mass_copy(d, c):
        to = zpeer(d)
        return pltpu.make_async_remote_copy(
            src_ref=stage.at[c, pl.ds(pl.multiple_of(to * share, share), share)], dst_ref=landed.at[c, nz - d],
            send_sem=zsend_sem.at[d, c], recv_sem=zrecv_sem.at[nz - d, c],
            device_id={"ref": to}, device_id_type=MESH,
        )

    for d in range(1, nz):
        stat_copy(d).start()

    def mass_step(c, carry):
        def far_labels(d, carry):
            arrived_lab(cores * d, c)
            if cores == 2:
                pass_lab(d, c).start()
            return carry

        lax.fori_loop(1, ny, far_labels, 0)
        pltpu.make_async_copy(lab_piece(0, c), lab_piece(0, c), own_sem.at[nr + c]).wait()
        if cores == 2:

            def other_labels(d, carry):
                arrived_lab(cores * d + 1, c)
                return carry

            lax.fori_loop(0, ny, other_labels, 0)
        part = jnp.dot(wts[...], labs[c], preferred_element_type=jnp.float32)
        mass[c] = part
        stage[c] = part.astype(jnp.bfloat16)
        for d in range(1, nz):
            mass_copy(d, c).start()
        return carry

    lax.fori_loop(0, nc, mass_step, 0)

    mine = pl.ds(pl.multiple_of(zi * share, share), share)

    def spread(d, row):
        line = stat_in[d, row:row + 1, :] if d else None
        if d == 0:
            line = stat_out[row:row + 1, mine] if narrow else stat_out[row:row + 1, :]
        full = jnp.broadcast_to(line, (LANES, line.shape[1])).T
        if narrow:
            return full
        wide[...] = full
        return wide[mine, :]

    for d in range(1, nz):
        stat_copy(nz - d).wait_recv()
    tops = [spread(d, 0) for d in range(nz)]
    top = functools.reduce(jnp.maximum, tops)
    shrinks = [jnp.exp(t - top) for t in tops]
    total = sum(f * spread(d, 4) for d, f in enumerate(shrinks))
    log_total = jnp.log(total)

    for c in range(nc):
        acc = mass[c, mine, :] * shrinks[0]
        for d in range(1, nz):
            mass_copy(nz - d, c).wait_recv()
            acc += landed[c, d].astype(jnp.float32) * shrinks[d]
        out_ref[:, c * LANES:(c + 1) * LANES] = jnp.log(acc) - log_total

    for d in range(1, nz):
        stat_copy(d).wait_send()
        for c in range(nc):
            mass_copy(d, c).wait_send()
    for d in range(1, ny):
        for j in range(nr):
            to_peer_ref(d, j).wait_send()
            if cores == 2:
                pass_ref(d, j).wait_send()
        for c in range(nc):
            to_peer_lab(d, c).wait_send()
            if cores == 2:
                pass_lab(d, c).wait_send()
    if cores == 2:
        for j in range(nr):
            to_sib_ref(j).wait_send()
        for c in range(nc):
            to_sib_lab(c).wait_send()


def per_device(queries, references, labels):
    nq, width = queries.shape
    rows = references.shape[0]
    classes = labels.shape[1]
    nb, nz = lax.axis_size("blk"), lax.axis_size("ref")
    cores = 2 if nb % 2 == 0 else 1
    ny = nb // cores
    share = nq // nz
    nr, nc = rows // LANES, classes // LANES
    items = nr + nc
    score_scale = 2.0 / math.sqrt(width)
    stat_w = share if share % LANES == 0 else nq
    return pl.pallas_call(
        functools.partial(kernel, ny, cores, nz, score_scale),
        out_shape=jax.ShapeDtypeStruct((share, classes), jnp.float32),
        in_specs=[pl.BlockSpec(memory_space=pltpu.HBM)] * 3,
        out_specs=pl.BlockSpec(memory_space=pltpu.VMEM),
        scratch_shapes=[
            pltpu.VMEM((nq, width), jnp.bfloat16),
            pltpu.VMEM((nb, rows, width), jnp.bfloat16),
            pltpu.VMEM((nc, nb * rows, LANES), jnp.bfloat16),
            pltpu.VMEM((nb * nr, nq, LANES), jnp.float32),
            pltpu.VMEM((nq, LANES), jnp.float32),
            pltpu.VMEM((nq, nb * rows), jnp.bfloat16),
            pltpu.VMEM((nc, nq, LANES), jnp.float32),
            pltpu.VMEM((nc, nq, LANES), jnp.bfloat16),
            pltpu.VMEM((nc, nz, share, LANES), jnp.bfloat16),
            pltpu.VMEM((8, nq), jnp.float32),
            pltpu.VMEM((nz, 8, stat_w), jnp.float32),
            pltpu.VMEM((nq, LANES), jnp.float32),
            pltpu.SemaphoreType.DMA,
            pltpu.SemaphoreType.DMA((items,)),
            pltpu.SemaphoreType.DMA((nb, items)),
            pltpu.SemaphoreType.DMA((nb, items)),
            pltpu.SemaphoreType.DMA((nz, nc)),
            pltpu.SemaphoreType.DMA((nz, nc)),
            pltpu.SemaphoreType.DMA((nz,)),
            pltpu.SemaphoreType.DMA((nz,)),
        ],
        compiler_params=pltpu.CompilerParams(
            collective_id=0, has_side_effects=True, vmem_limit_bytes=VMEM_LIMIT
        ),
    )(queries, references, labels)


def solution(mesh):
    return jax.shard_map(
        per_device,
        mesh=mesh,
        in_specs=(
            P(("groups", "blk"), None),
            P(("groups", "blk", "ref"), None),
            P(("groups", "blk", "ref"), None),
        ),
        out_specs=P(("groups", "blk", "ref"), None),
        check_vma=False,
    )
```

```python
import functools
import math

import jax
import jax.numpy as jnp
from jax import lax
from jax.experimental import pallas as pl
from jax.experimental.pallas import tpu as pltpu
from jax.sharding import PartitionSpec as P

MESH = pl.DeviceIdType.MESH
LANES = 128
VMEM_LIMIT = 64 * 1024 * 1024 - 256 * 1024


def kernel(
    ny, cores, nz, score_scale,
    q_hbm, r_hbm, l_hbm, out_ref,
    q, refs, labs, scores, peak, wts, mass, stage, stage_mid, landed, stat_out, stat_mid, stat_in, wide,
    q_sem, own_sem, send_sem, recv_sem, zsend_sem, zrecv_sem, tsend_sem, trecv_sem,
):
    blk = lax.axis_index("blk")
    zi = lax.axis_index("ref")
    nb = ny * cores
    rows, width = r_hbm.shape
    classes = l_hbm.shape[1]
    nq = q_hbm.shape[0]
    share = nq // nz
    nr = rows // LANES
    nc = classes // LANES
    items = nr + nc
    yi, core = blk // cores, blk % cores
    sibling = yi * cores + (1 - core)

    def peer(d):
        return ((yi + d) % ny) * cores + core

    def zpeer(d):
        return (zi + d) % nz

    def ref_piece(slot, j):
        return refs.at[slot, pl.ds(pl.multiple_of(j * LANES, LANES), LANES)]

    def lab_piece(slot, c):
        return labs.at[c, pl.ds(pl.multiple_of(slot * rows, rows), rows)]

    def own_ref(j):
        return r_hbm.at[pl.ds(j * LANES, LANES)]

    def own_lab(c):
        return l_hbm.at[:, pl.ds(c * LANES, LANES)]

    def remote(src, dst, sent, slot, item, dev):
        return pltpu.make_async_remote_copy(
            src_ref=src, dst_ref=dst, send_sem=send_sem.at[sent, item], recv_sem=recv_sem.at[slot, item],
            device_id={"blk": dev}, device_id_type=MESH,
        )

    def to_peer_ref(d, j):
        slot = cores * (ny - d)
        return remote(own_ref(j), ref_piece(slot, j), cores * d, slot, j, peer(d))

    def to_peer_lab(d, c):
        slot = cores * (ny - d)
        return remote(own_lab(c), lab_piece(slot, c), cores * d, slot, nr + c, peer(d))

    def to_sib_ref(j):
        return remote(own_ref(j), ref_piece(1, j), 1, 1, j, sibling)

    def to_sib_lab(c):
        return remote(own_lab(c), lab_piece(1, c), 1, 1, nr + c, sibling)

    def pass_ref(d, j):
        return remote(ref_piece(cores * d, j), ref_piece(cores * d + 1, j), cores * d + 1, cores * d + 1, j, sibling)

    def pass_lab(d, c):
        return remote(lab_piece(cores * d, c), lab_piece(cores * d + 1, c), cores * d + 1, cores * d + 1, nr + c, sibling)

    def arrived_ref(slot, j):
        remote(ref_piece(slot, j), ref_piece(slot, j), slot, slot, j, sibling).wait_recv()

    def arrived_lab(slot, c):
        remote(lab_piece(slot, c), lab_piece(slot, c), slot, slot, nr + c, sibling).wait_recv()

    q_copy = pltpu.make_async_copy(q_hbm, q, q_sem)
    q_copy.start()
    own_copies = [pltpu.make_async_copy(own_ref(j), ref_piece(0, j), own_sem.at[j]) for j in range(nr)]
    own_copies += [pltpu.make_async_copy(own_lab(c), lab_piece(0, c), own_sem.at[nr + c]) for c in range(nc)]
    for copy in own_copies:
        copy.start()

    barrier = pltpu.get_barrier_semaphore()
    if cores == 2:
        pl.semaphore_signal(barrier, inc=1, device_id={"blk": sibling}, device_id_type=MESH)
    for d in range(1, ny):
        pl.semaphore_signal(barrier, inc=1, device_id={"blk": peer(d)}, device_id_type=MESH)
    for d in range(1, nz):
        pl.semaphore_signal(barrier, inc=1, device_id={"ref": zpeer(d)}, device_id_type=MESH)
    pl.semaphore_wait(barrier, cores - 1 + ny - 1 + nz - 1)

    for j in range(nr):
        for d in range(1, ny):
            to_peer_ref(d, j).start()
    if cores == 2:
        for j in range(nr):
            to_sib_ref(j).start()
    for c in range(nc):
        for d in range(1, ny):
            to_peer_lab(d, c).start()
    if cores == 2:
        for c in range(nc):
            to_sib_lab(c).start()

    peak[...] = jnp.full(peak.shape, -jnp.inf, jnp.float32)

    def score(slot, j):
        part = lax.dot_general(
            q[...], ref_piece(slot, j)[...], (((1,), (1,)), ((), ())), preferred_element_type=jnp.float32
        ) * score_scale
        scores[slot * nr + j] = part
        peak[...] = jnp.maximum(peak[...], part)

    q_copy.wait()
    for j in range(nr):
        own_copies[j].wait()

    def own_step(j, carry):
        score(0, j)
        return carry

    lax.fori_loop(0, nr, own_step, 0)

    if cores == 2:

        def sib_step(j, carry):
            arrived_ref(1, j)
            score(1, j)
            return carry

        lax.fori_loop(0, nr, sib_step, 0)

    def far_step(i, carry):
        d, j = 1 + i // nr, i % nr
        arrived_ref(cores * d, j)
        if cores == 2:
            pass_ref(d, j).start()
        score(cores * d, j)
        if cores == 2:
            arrived_ref(cores * d + 1, j)
            score(cores * d + 1, j)
        return carry

    lax.fori_loop(0, (ny - 1) * nr, far_step, 0)

    lane = lax.broadcasted_iota(jnp.int32, (LANES, LANES), 1)

    def weigh(t, carry):
        r = pl.ds(pl.multiple_of(t * LANES, LANES), LANES)
        top = jnp.broadcast_to(jnp.max(peak[r, :], axis=1, keepdims=True), (LANES, LANES))

        def one(i, total):
            w = jnp.exp(scores[i, r, :] - top).astype(jnp.bfloat16)
            wts[r, pl.ds(pl.multiple_of(i * LANES, LANES), LANES)] = w
            return total + w.astype(jnp.float32)

        total = lax.fori_loop(0, nb * nr, one, jnp.zeros((LANES, LANES), jnp.float32), unroll=nb * nr <= 8)
        total = jnp.broadcast_to(jnp.sum(total, axis=1, keepdims=True), (LANES, LANES))
        stat_out[:, r] = jnp.where(lane < 4, top, total).T[0:8]
        return carry

    lax.fori_loop(0, nq // LANES, weigh, 0)

    narrow = share % LANES == 0

    merge = nz == 4 and narrow
    half = zi // 2
    mate = zi + 1 - 2 * (zi % 2)
    inner = 2 - half
    outer = 3 - 3 * half
    is_end = (zi + half + 1) % 2

    def rows_of(to):
        return pl.ds(pl.multiple_of(to * share, share), share)

    def stat_copy(src, kind, slot, to):
        return pltpu.make_async_remote_copy(
            src_ref=src, dst_ref=stat_in.at[slot], send_sem=tsend_sem.at[kind], recv_sem=trecv_sem.at[slot],
            device_id={"ref": to}, device_id_type=MESH,
        )

    def stat_rows(to):
        return stat_out.at[:, rows_of(to)] if narrow else stat_out

    def mass_copy(src, kind, slot, to, c):
        return pltpu.make_async_remote_copy(
            src_ref=src, dst_ref=landed.at[c, slot], send_sem=zsend_sem.at[kind, c], recv_sem=zrecv_sem.at[slot, c],
            device_id={"ref": to}, device_id_type=MESH,
        )

    if merge:
        plain = [(1, 1 + is_end, inner), (0, 0, mate)]
    else:
        plain = [(d, nz - d, zpeer(d)) for d in range(1, nz)]

    def stat_plain(kind, slot, to):
        return stat_copy(stat_rows(to), kind, slot, to)

    def mass_plain(kind, slot, to, c):
        return mass_copy(stage.at[c, rows_of(to)], kind, slot, to, c)

    def stat_via():
        return stat_copy(stat_rows(outer), 2, 3, mate)

    def mass_via(c):
        return mass_copy(stage.at[c, rows_of(outer)], 2, 3, mate, c)

    def stat_both():
        return stat_copy(stat_mid, 2, 1, outer)

    def mass_both(c):
        return mass_copy(stage_mid.at[c], 2, 1, outer, c)

    def stat_arrived(slot):
        stat_copy(stat_in.at[slot], 0, slot, mate if merge else zpeer(1)).wait_recv()

    def mass_arrived(slot, c):
        mass_copy(landed.at[c, slot], 0, slot, mate if merge else zpeer(1), c).wait_recv()

    def across(line):
        return jnp.broadcast_to(line, (LANES, line.shape[1])).T

    def join_stats():
        stat_arrived(3)
        here = stat_out[:, rows_of(outer)]
        there = stat_in[3]
        top = jnp.maximum(here[0:4], there[0:4])
        shrink_here = jnp.exp(here[0:4] - top)
        shrink_there = jnp.exp(there[0:4] - top)
        stat_mid[0:4, :] = top
        stat_mid[4:8, :] = here[4:8] * shrink_here + there[4:8] * shrink_there
        stat_both().start()
        wide[0:share, :] = across(shrink_here[0:1])
        wide[share:2 * share, :] = across(shrink_there[0:1])

    def join_mass(c):
        mass_arrived(3, c)
        both = mass[c, rows_of(outer), :] * wide[0:share, :]
        both += landed[c, 3].astype(jnp.float32) * wide[share:2 * share, :]
        stage_mid[c] = both.astype(jnp.bfloat16)
        mass_both(c).start()

    if merge:
        pl.when(is_end == 1)(lambda: stat_via().start())
    for to in plain:
        stat_plain(*to).start()

    for c in range(nc):

        def far_labels(d, carry):
            arrived_lab(cores * d, c)
            if cores == 2:
                pass_lab(d, c).start()
            return carry

        lax.fori_loop(1, ny, far_labels, 0)
        own_copies[nr + c].wait()
        if cores == 2:

            def other_labels(d, carry):
                arrived_lab(cores * d + 1, c)
                return carry

            lax.fori_loop(0, ny, other_labels, 0)
        part = jnp.dot(wts[...], labs[c], preferred_element_type=jnp.float32)
        mass[c] = part
        stage[c] = part.astype(jnp.bfloat16)
        if merge:
            pl.when(is_end == 1)(lambda: mass_via(c).start())
        for to in plain:
            mass_plain(*to, c).start()
        if merge:

            @pl.when(is_end == 0)
            def _():
                if c == 0:
                    join_stats()
                else:
                    join_mass(c - 1)
                if c == nc - 1:
                    join_mass(c)

    mine = rows_of(zi)

    def spread(slot, row):
        if slot is None:
            line = stat_out[row:row + 1, mine] if narrow else stat_out[row:row + 1, :]
        else:
            line = stat_in[slot, row:row + 1, :]
        full = across(line)
        if narrow:
            return full
        wide[...] = full
        return wide[mine, :]

    def finish(slots):
        for slot in slots:
            stat_arrived(slot)
        senders = [None] + slots
        tops = [spread(slot, 0) for slot in senders]
        top = functools.reduce(jnp.maximum, tops)
        shrinks = [jnp.exp(t - top) for t in tops]
        total = sum(f * spread(slot, 4) for slot, f in zip(senders, shrinks))
        log_total = jnp.log(total)
        for c in range(nc):
            acc = mass[c, mine, :] * shrinks[0]
            for slot, f in zip(slots, shrinks[1:]):
                mass_arrived(slot, c)
                acc += landed[c, slot].astype(jnp.float32) * f
            out_ref[:, c * LANES:(c + 1) * LANES] = jnp.log(acc) - log_total

    if merge:

        @pl.when(is_end == 1)
        def _():
            finish([0, 1])
            stat_via().wait_send()
            for c in range(nc):
                mass_via(c).wait_send()

        @pl.when(is_end == 0)
        def _():
            finish([0, 1, 2])
            stat_both().wait_send()
            for c in range(nc):
                mass_both(c).wait_send()
    else:
        finish(list(range(1, nz)))

    for to in plain:
        stat_plain(*to).wait_send()
        for c in range(nc):
            mass_plain(*to, c).wait_send()
    for d in range(1, ny):
        for j in range(nr):
            to_peer_ref(d, j).wait_send()
            if cores == 2:
                pass_ref(d, j).wait_send()
        for c in range(nc):
            to_peer_lab(d, c).wait_send()
            if cores == 2:
                pass_lab(d, c).wait_send()
    if cores == 2:
        for j in range(nr):
            to_sib_ref(j).wait_send()
        for c in range(nc):
            to_sib_lab(c).wait_send()


def per_device(queries, references, labels):
    nq, width = queries.shape
    rows = references.shape[0]
    classes = labels.shape[1]
    nb, nz = lax.axis_size("blk"), lax.axis_size("ref")
    cores = 2 if nb % 2 == 0 else 1
    ny = nb // cores
    share = nq // nz
    nr, nc = rows // LANES, classes // LANES
    items = nr + nc
    score_scale = 2.0 / math.sqrt(width)
    stat_w = share if share % LANES == 0 else nq
    return pl.pallas_call(
        functools.partial(kernel, ny, cores, nz, score_scale),
        out_shape=jax.ShapeDtypeStruct((share, classes), jnp.float32),
        in_specs=[pl.BlockSpec(memory_space=pltpu.HBM)] * 3,
        out_specs=pl.BlockSpec(memory_space=pltpu.VMEM),
        scratch_shapes=[
            pltpu.VMEM((nq, width), jnp.bfloat16),
            pltpu.VMEM((nb, rows, width), jnp.bfloat16),
            pltpu.VMEM((nc, nb * rows, LANES), jnp.bfloat16),
            pltpu.VMEM((nb * nr, nq, LANES), jnp.float32),
            pltpu.VMEM((nq, LANES), jnp.float32),
            pltpu.VMEM((nq, nb * rows), jnp.bfloat16),
            pltpu.VMEM((nc, nq, LANES), jnp.float32),
            pltpu.VMEM((nc, nq, LANES), jnp.bfloat16),
            pltpu.VMEM((nc, share, LANES), jnp.bfloat16),
            pltpu.VMEM((nc, nz, share, LANES), jnp.bfloat16),
            pltpu.VMEM((8, nq), jnp.float32),
            pltpu.VMEM((8, stat_w), jnp.float32),
            pltpu.VMEM((nz, 8, stat_w), jnp.float32),
            pltpu.VMEM((nq, LANES), jnp.float32),
            pltpu.SemaphoreType.DMA,
            pltpu.SemaphoreType.DMA((items,)),
            pltpu.SemaphoreType.DMA((nb, items)),
            pltpu.SemaphoreType.DMA((nb, items)),
            pltpu.SemaphoreType.DMA((nz, nc)),
            pltpu.SemaphoreType.DMA((nz, nc)),
            pltpu.SemaphoreType.DMA((nz,)),
            pltpu.SemaphoreType.DMA((nz,)),
        ],
        compiler_params=pltpu.CompilerParams(
            collective_id=0, has_side_effects=True, vmem_limit_bytes=VMEM_LIMIT
        ),
    )(queries, references, labels)


def solution(mesh):
    return jax.shard_map(
        per_device,
        mesh=mesh,
        in_specs=(
            P(("groups", "blk"), None),
            P(("groups", "blk", "ref"), None),
            P(("groups", "blk", "ref"), None),
        ),
        out_specs=P(("groups", "blk", "ref"), None),
        check_vma=False,
    )
```

```python
import functools
import math

import jax
import jax.numpy as jnp
from jax import lax
from jax.experimental import pallas as pl
from jax.experimental.pallas import tpu as pltpu
from jax.sharding import PartitionSpec as P

MESH = pl.DeviceIdType.MESH
LANES = 128
VMEM_LIMIT = 64 * 1024 * 1024 - 256 * 1024


def kernel(
    ny, cores, nz, score_scale,
    q_hbm, r_hbm, l_hbm, out_ref,
    q, refs, labs, scores, peak, first, wts, mass, stage, stage_mid, landed, stat_out, stat_mid, stat_in, wide,
    q_sem, own_sem, send_sem, recv_sem, zsend_sem, zrecv_sem, tsend_sem, trecv_sem,
):
    blk = lax.axis_index("blk")
    zi = lax.axis_index("ref")
    nb = ny * cores
    rows, width = r_hbm.shape
    classes = l_hbm.shape[1]
    nq = q_hbm.shape[0]
    share = nq // nz
    nr = rows // LANES
    nc = classes // LANES
    items = nr + nc
    yi, core = blk // cores, blk % cores
    sibling = yi * cores + (1 - core)

    def peer(d):
        return ((yi + d) % ny) * cores + core

    def zpeer(d):
        return (zi + d) % nz

    def ref_piece(slot, j):
        return refs.at[slot, pl.ds(pl.multiple_of(j * LANES, LANES), LANES)]

    def lab_piece(slot, c):
        return labs.at[c, pl.ds(pl.multiple_of(slot * rows, rows), rows)]

    def own_ref(j):
        return r_hbm.at[pl.ds(j * LANES, LANES)]

    def own_lab(c):
        return l_hbm.at[:, pl.ds(c * LANES, LANES)]

    def remote(src, dst, sent, slot, item, dev):
        return pltpu.make_async_remote_copy(
            src_ref=src, dst_ref=dst, send_sem=send_sem.at[sent, item], recv_sem=recv_sem.at[slot, item],
            device_id={"blk": dev}, device_id_type=MESH,
        )

    def to_peer_ref(d, j):
        slot = cores * (ny - d)
        return remote(own_ref(j), ref_piece(slot, j), cores * d, slot, j, peer(d))

    def to_peer_lab(d, c):
        slot = cores * (ny - d)
        return remote(own_lab(c), lab_piece(slot, c), cores * d, slot, nr + c, peer(d))

    def to_sib_ref(j):
        return remote(own_ref(j), ref_piece(1, j), 1, 1, j, sibling)

    def to_sib_lab(c):
        return remote(own_lab(c), lab_piece(1, c), 1, 1, nr + c, sibling)

    def pass_ref(d, j):
        return remote(ref_piece(cores * d, j), ref_piece(cores * d + 1, j), cores * d + 1, cores * d + 1, j, sibling)

    def pass_lab(d, c):
        return remote(lab_piece(cores * d, c), lab_piece(cores * d + 1, c), cores * d + 1, cores * d + 1, nr + c, sibling)

    def arrived_ref(slot, j):
        remote(ref_piece(slot, j), ref_piece(slot, j), slot, slot, j, sibling).wait_recv()

    def arrived_lab(slot, c):
        remote(lab_piece(slot, c), lab_piece(slot, c), slot, slot, nr + c, sibling).wait_recv()

    q_copy = pltpu.make_async_copy(q_hbm, q, q_sem)
    q_copy.start()
    own_copies = [pltpu.make_async_copy(own_ref(j), ref_piece(0, j), own_sem.at[j]) for j in range(nr)]
    own_copies += [pltpu.make_async_copy(own_lab(c), lab_piece(0, c), own_sem.at[nr + c]) for c in range(nc)]
    for copy in own_copies:
        copy.start()

    barrier = pltpu.get_barrier_semaphore()
    if cores == 2:
        pl.semaphore_signal(barrier, inc=1, device_id={"blk": sibling}, device_id_type=MESH)
    for d in range(1, ny):
        pl.semaphore_signal(barrier, inc=1, device_id={"blk": peer(d)}, device_id_type=MESH)
    for d in range(1, nz):
        pl.semaphore_signal(barrier, inc=1, device_id={"ref": zpeer(d)}, device_id_type=MESH)
    pl.semaphore_wait(barrier, cores - 1 + ny - 1 + nz - 1)

    for j in range(nr):
        for d in range(1, ny):
            to_peer_ref(d, j).start()
    if cores == 2:
        for j in range(nr):
            to_sib_ref(j).start()
    for c in range(nc):
        for d in range(1, ny):
            to_peer_lab(d, c).start()
    if cores == 2:
        for c in range(nc):
            to_sib_lab(c).start()

    peak[...] = jnp.full(peak.shape, -jnp.inf, jnp.float32)

    def score(slot, j):
        part = lax.dot_general(
            q[...], ref_piece(slot, j)[...], (((1,), (1,)), ((), ())), preferred_element_type=jnp.float32
        ) * score_scale
        scores[slot * nr + j] = part
        peak[...] = jnp.maximum(peak[...], part)

    q_copy.wait()
    for j in range(nr):
        own_copies[j].wait()

    def own_step(j, carry):
        score(0, j)
        return carry

    lax.fori_loop(0, nr, own_step, 0)

    if cores == 2:

        def sib_step(j, carry):
            arrived_ref(1, j)
            score(1, j)
            return carry

        lax.fori_loop(0, nr, sib_step, 0)

    lane = lax.broadcasted_iota(jnp.int32, (LANES, LANES), 1)
    near = cores * nr

    def tile(t):
        return pl.ds(pl.multiple_of(t * LANES, LANES), LANES)

    def weights_of(r, low, high):
        top = jnp.broadcast_to(jnp.max(peak[r, :], axis=1, keepdims=True), (LANES, LANES))

        def one(i, total):
            w = jnp.exp(scores[i, r, :] - top).astype(jnp.bfloat16)
            wts[r, pl.ds(pl.multiple_of(i * LANES, LANES), LANES)] = w
            return total + w.astype(jnp.float32)

        total = lax.fori_loop(low, high, one, jnp.zeros((LANES, LANES), jnp.float32), unroll=high - low <= 8)
        return top, jnp.broadcast_to(jnp.sum(total, axis=1, keepdims=True), (LANES, LANES))

    def weigh_near(t, carry):
        r = tile(t)
        top, total = weights_of(r, 0, near)
        first[0, r, :] = top
        first[1, r, :] = total
        if ny == 1:
            stat_out[:, r] = jnp.where(lane < 4, top, total).T[0:8]
        return carry

    def weigh_far(t, carry):
        r = tile(t)
        top, total = weights_of(r, near, nb * nr)
        shrink = jnp.exp(first[0, r, :] - top)
        first[0, r, :] = shrink
        total += first[1, r, :] * shrink
        stat_out[:, r] = jnp.where(lane < 4, top, total).T[0:8]
        return carry

    lax.fori_loop(0, nq // LANES, weigh_near, 0)

    def far_step(i, carry):
        d, j = 1 + i // nr, i % nr
        arrived_ref(cores * d, j)
        if cores == 2:
            pass_ref(d, j).start()
        score(cores * d, j)
        if cores == 2:
            arrived_ref(cores * d + 1, j)
            score(cores * d + 1, j)
        return carry

    lax.fori_loop(0, (ny - 1) * nr, far_step, 0)

    def far_labels(c):
        def one(d, carry):
            arrived_lab(cores * d, c)
            if cores == 2:
                pass_lab(d, c).start()
            return carry

        lax.fori_loop(1, ny, one, 0)

    far_labels(0)
    if ny > 1:
        lax.fori_loop(0, nq // LANES, weigh_far, 0)

    narrow = share % LANES == 0

    merge = nz == 4 and narrow
    half = zi // 2
    mate = zi + 1 - 2 * (zi % 2)
    inner = 2 - half
    outer = 3 - 3 * half
    is_end = (zi + half + 1) % 2

    def rows_of(to):
        return pl.ds(pl.multiple_of(to * share, share), share)

    def stat_copy(src, kind, slot, to):
        return pltpu.make_async_remote_copy(
            src_ref=src, dst_ref=stat_in.at[slot], send_sem=tsend_sem.at[kind], recv_sem=trecv_sem.at[slot],
            device_id={"ref": to}, device_id_type=MESH,
        )

    def stat_rows(to):
        return stat_out.at[:, rows_of(to)] if narrow else stat_out

    def mass_copy(src, kind, slot, to, c):
        return pltpu.make_async_remote_copy(
            src_ref=src, dst_ref=landed.at[c, slot], send_sem=zsend_sem.at[kind, c], recv_sem=zrecv_sem.at[slot, c],
            device_id={"ref": to}, device_id_type=MESH,
        )

    if merge:
        plain = [(1, 1 + is_end, inner), (0, 0, mate)]
    else:
        plain = [(d, nz - d, zpeer(d)) for d in range(1, nz)]

    def stat_plain(kind, slot, to):
        return stat_copy(stat_rows(to), kind, slot, to)

    def mass_plain(kind, slot, to, c):
        return mass_copy(stage.at[c, rows_of(to)], kind, slot, to, c)

    def stat_via():
        return stat_copy(stat_rows(outer), 2, 3, mate)

    def mass_via(c):
        return mass_copy(stage.at[c, rows_of(outer)], 2, 3, mate, c)

    def stat_both():
        return stat_copy(stat_mid, 2, 1, outer)

    def mass_both(c):
        return mass_copy(stage_mid.at[c], 2, 1, outer, c)

    def stat_arrived(slot):
        stat_copy(stat_in.at[slot], 0, slot, mate if merge else zpeer(1)).wait_recv()

    def mass_arrived(slot, c):
        mass_copy(landed.at[c, slot], 0, slot, mate if merge else zpeer(1), c).wait_recv()

    def across(line):
        return jnp.broadcast_to(line, (LANES, line.shape[1])).T

    def join_stats():
        stat_arrived(3)
        here = stat_out[:, rows_of(outer)]
        there = stat_in[3]
        top = jnp.maximum(here[0:4], there[0:4])
        shrink_here = jnp.exp(here[0:4] - top)
        shrink_there = jnp.exp(there[0:4] - top)
        stat_mid[0:4, :] = top
        stat_mid[4:8, :] = here[4:8] * shrink_here + there[4:8] * shrink_there
        stat_both().start()
        wide[0:share, :] = across(shrink_here[0:1])
        wide[share:2 * share, :] = across(shrink_there[0:1])

    def join_mass(c):
        mass_arrived(3, c)
        both = mass[c, rows_of(outer), :] * wide[0:share, :]
        both += landed[c, 3].astype(jnp.float32) * wide[share:2 * share, :]
        stage_mid[c] = both.astype(jnp.bfloat16)
        mass_both(c).start()

    if merge:
        pl.when(is_end == 1)(lambda: stat_via().start())
    for to in plain:
        stat_plain(*to).start()

    for c in range(nc):

        if c > 0:
            far_labels(c)
        own_copies[nr + c].wait()
        if cores == 2:

            def other_labels(d, carry):
                arrived_lab(cores * d + 1, c)
                return carry

            lax.fori_loop(0, ny, other_labels, 0)
        split = cores * rows
        part = jnp.dot(wts[:, 0:split], labs[c, 0:split, :], preferred_element_type=jnp.float32)
        if ny > 1:
            part = part * first[0] + jnp.dot(
                wts[:, split:], labs[c, split:, :], preferred_element_type=jnp.float32
            )
        mass[c] = part
        stage[c] = part.astype(jnp.bfloat16)
        if merge:
            pl.when(is_end == 1)(lambda: mass_via(c).start())
        for to in plain:
            mass_plain(*to, c).start()
        if merge:

            @pl.when(is_end == 0)
            def _():
                if c == 0:
                    join_stats()
                else:
                    join_mass(c - 1)
                if c == nc - 1:
                    join_mass(c)

    mine = rows_of(zi)

    def spread(slot, row):
        if slot is None:
            line = stat_out[row:row + 1, mine] if narrow else stat_out[row:row + 1, :]
        else:
            line = stat_in[slot, row:row + 1, :]
        full = across(line)
        if narrow:
            return full
        wide[...] = full
        return wide[mine, :]

    def finish(slots):
        for slot in slots:
            stat_arrived(slot)
        senders = [None] + slots
        tops = [spread(slot, 0) for slot in senders]
        top = functools.reduce(jnp.maximum, tops)
        shrinks = [jnp.exp(t - top) for t in tops]
        total = sum(f * spread(slot, 4) for slot, f in zip(senders, shrinks))
        log_total = jnp.log(total)
        for c in range(nc):
            acc = mass[c, mine, :] * shrinks[0]
            for slot, f in zip(slots, shrinks[1:]):
                mass_arrived(slot, c)
                acc += landed[c, slot].astype(jnp.float32) * f
            out_ref[:, c * LANES:(c + 1) * LANES] = jnp.log(acc) - log_total

    if merge:

        @pl.when(is_end == 1)
        def _():
            finish([0, 1])
            stat_via().wait_send()
            for c in range(nc):
                mass_via(c).wait_send()

        @pl.when(is_end == 0)
        def _():
            finish([0, 1, 2])
            stat_both().wait_send()
            for c in range(nc):
                mass_both(c).wait_send()
    else:
        finish(list(range(1, nz)))

    for to in plain:
        stat_plain(*to).wait_send()
        for c in range(nc):
            mass_plain(*to, c).wait_send()
    for d in range(1, ny):
        for j in range(nr):
            to_peer_ref(d, j).wait_send()
            if cores == 2:
                pass_ref(d, j).wait_send()
        for c in range(nc):
            to_peer_lab(d, c).wait_send()
            if cores == 2:
                pass_lab(d, c).wait_send()
    if cores == 2:
        for j in range(nr):
            to_sib_ref(j).wait_send()
        for c in range(nc):
            to_sib_lab(c).wait_send()


def per_device(queries, references, labels):
    nq, width = queries.shape
    rows = references.shape[0]
    classes = labels.shape[1]
    nb, nz = lax.axis_size("blk"), lax.axis_size("ref")
    cores = 2 if nb % 2 == 0 else 1
    ny = nb // cores
    share = nq // nz
    nr, nc = rows // LANES, classes // LANES
    items = nr + nc
    score_scale = 2.0 / math.sqrt(width)
    stat_w = share if share % LANES == 0 else nq
    return pl.pallas_call(
        functools.partial(kernel, ny, cores, nz, score_scale),
        out_shape=jax.ShapeDtypeStruct((share, classes), jnp.float32),
        in_specs=[pl.BlockSpec(memory_space=pltpu.HBM)] * 3,
        out_specs=pl.BlockSpec(memory_space=pltpu.VMEM),
        scratch_shapes=[
            pltpu.VMEM((nq, width), jnp.bfloat16),
            pltpu.VMEM((nb, rows, width), jnp.bfloat16),
            pltpu.VMEM((nc, nb * rows, LANES), jnp.bfloat16),
            pltpu.VMEM((nb * nr, nq, LANES), jnp.float32),
            pltpu.VMEM((nq, LANES), jnp.float32),
            pltpu.VMEM((2, nq, LANES), jnp.float32),
            pltpu.VMEM((nq, nb * rows), jnp.bfloat16),
            pltpu.VMEM((nc, nq, LANES), jnp.float32),
            pltpu.VMEM((nc, nq, LANES), jnp.bfloat16),
            pltpu.VMEM((nc, share, LANES), jnp.bfloat16),
            pltpu.VMEM((nc, nz, share, LANES), jnp.bfloat16),
            pltpu.VMEM((8, nq), jnp.float32),
            pltpu.VMEM((8, stat_w), jnp.float32),
            pltpu.VMEM((nz, 8, stat_w), jnp.float32),
            pltpu.VMEM((nq, LANES), jnp.float32),
            pltpu.SemaphoreType.DMA,
            pltpu.SemaphoreType.DMA((items,)),
            pltpu.SemaphoreType.DMA((nb, items)),
            pltpu.SemaphoreType.DMA((nb, items)),
            pltpu.SemaphoreType.DMA((nz, nc)),
            pltpu.SemaphoreType.DMA((nz, nc)),
            pltpu.SemaphoreType.DMA((nz,)),
            pltpu.SemaphoreType.DMA((nz,)),
        ],
        compiler_params=pltpu.CompilerParams(
            collective_id=0, has_side_effects=True, vmem_limit_bytes=VMEM_LIMIT
        ),
    )(queries, references, labels)


def solution(mesh):
    return jax.shard_map(
        per_device,
        mesh=mesh,
        in_specs=(
            P(("groups", "blk"), None),
            P(("groups", "blk", "ref"), None),
            P(("groups", "blk", "ref"), None),
        ),
        out_specs=P(("groups", "blk", "ref"), None),
        check_vma=False,
    )
```
